768 devices in a mesh: loop: 8 (over z_hi, core), rep: 96 (over x, y, z_lo).
Axes of the slice: x: 4, y: 8, z: 12 (z_hi: 4, z_lo: 3; z = z_hi * 3 + z_lo), core: 2. Of those that a mesh axis runs over, the one named last changes fastest.
Arguments:
- features: float32 [196608, 256], P(('loop', 'rep')), may hold values from -6 to 6
- weight: float32 [256, 256], replicated, may hold values from -0.375 to 0.375
- bias: float32 [256], replicated, may hold values from -3 to 3
- tile_values: float32 [768, 32, 128, 128], P(('loop', 'rep')), may hold values from -0.125 to 0.125
- tile_rows: int32 [768, 32], P(('loop', 'rep')), may hold values from 0 to 9
- tile_cols: int32 [768, 32], P(('loop', 'rep')), may hold values from 0 to 1
- tile_counts: int32 [768, 8], P(('loop', 'rep')), may hold values from 1 to 4, as said below
- cotangent: float32 [196608, 256], P(('loop', 'rep')), may hold values from -60 to 60
Outputs:
- output: float32 [196608, 256], P(('loop', 'rep'))
- grad_features: float32 [196608, 256], P(('loop', 'rep'))
- grad_weight: float32 [256, 256], replicated
- grad_bias: float32 [256], replicated
The draws below stay inside these ranges and needn't reach their ends.
Inputs may be any that keep to these rules, and one draw needn't show every extreme that they name: `tile_counts`: every entry is at least 1 and at most 4; 4 is reached in every draw. `tile_rows`: within one device, two live slots may name the same tile place; such tiles add.
All inputs are finite; a program needn't handle non-finite values.
Results may differ from the reference program's by a relative error of at most 0.00013.
Values sent between devices are 32-bit elements; how exact they have to be, the bound alone decides.
No kernel may reach another device: no remote copies, remote signals or barrier semaphores. Data moves between devices by JAX's collectives and lax.ppermute only.
A program may use at most 32 MiB of HBM per device.

```python
import jax
import jax.numpy as jnp
from jax import lax

H = 256
TILE = 128
ROWS = 256
KB = 4
BAND = 2
SLOTS = 32
NODES = 196608
N_LOOP = 8
N_REP = 96


def draw_tile_counts(key, part):
    key = jax.random.fold_in(key, 11)
    devices_all = N_LOOP * N_REP
    counts = jax.random.randint(jax.random.fold_in(key, 1), (devices_all * N_LOOP,), 1, KB + 1, dtype=jnp.int32)
    where_full = jax.random.randint(jax.random.fold_in(key, 2), (), 0, devices_all * N_LOOP, dtype=jnp.int32)
    flat_counts = jnp.where(jnp.arange(devices_all * N_LOOP, dtype=jnp.int32) == where_full, KB, counts)
    return flat_counts.reshape(devices_all, N_LOOP).astype(jnp.int32)


def draw_cotangent(key, part):
    key = jax.random.fold_in(key, 23)
    row_scale = jnp.exp(jax.random.uniform(jax.random.fold_in(key, 2), (NODES, 1), jnp.float32, 0.0, 2.302585))
    rising = 3.0 ** (jnp.arange(NODES, dtype=jnp.float32)[:, None] / (NODES - 1))
    noise = jnp.clip(jax.random.normal(jax.random.fold_in(key, 1), (NODES, H), jnp.float32), -6.0, 6.0)
    return (noise * row_scale * rising / 3.0).astype(jnp.float32)


def touch_ends(drawn, key, low, high):
    longest = drawn.shape.index(max(drawn.shape))
    spots = []
    for shift in (0, 1):
        where = [jax.random.randint(jax.random.fold_in(key, axis), (), 0, length) for axis, length in enumerate(drawn.shape)]
        where[longest] = (where[longest] + shift) % drawn.shape[longest]
        spots.append(tuple(where))
    return drawn.at[spots[0]].set(low).at[spots[1]].set(high)


def level_of(key, dims, pieces, least, top_value):
    gain = 1.0
    for position, blocks in pieces:
        steps = jax.random.uniform(jax.random.fold_in(jax.random.fold_in(key, 6), position), (blocks,), jnp.float32, least / len(pieces), top_value / len(pieces))
        gain = gain * jnp.repeat(jnp.exp(steps), dims[position] // blocks).reshape((-1,) + (1,) * (len(dims) - 1 - position))
    return gain


def bell_draw(own_key, extent, scale, most, split=(), kind=jnp.bfloat16):
    loudness = level_of(own_key, extent, split, -0.22, 0.18) if split else 1.0
    drawn = jax.random.normal(own_key, extent, jnp.float32) * scale * loudness
    return jnp.minimum(jnp.maximum(drawn, -most), most).astype(kind)


def setup_inputs(seed: int = 0) -> dict:
    arg_keys = jax.random.split(jax.random.key(seed), 9)
    features = bell_draw(arg_keys[0], (NODES, H), 1.0, 6.0, ((0, 768),), jnp.float32)
    weight = bell_draw(arg_keys[1], (H, H), H ** -0.5, 0.375, (), jnp.float32)
    bias = bell_draw(arg_keys[2], (H,), 0.5, 3.0, (), jnp.float32)
    tile_values = bell_draw(arg_keys[3], (N_LOOP * N_REP, SLOTS, TILE, TILE), (SLOTS * TILE * TILE // ROWS) ** -0.5, 0.125, ((0, 768),), jnp.float32)
    tile_rows = touch_ends(jax.random.randint(arg_keys[4], (N_LOOP * N_REP, SLOTS), 0, (2 * BAND + 1) * ROWS // TILE), jax.random.fold_in(arg_keys[4], 1), 0, ((2 * BAND + 1) * ROWS // TILE) - 1).astype(jnp.int32)
    tile_cols = touch_ends(jax.random.randint(arg_keys[5], (N_LOOP * N_REP, SLOTS), 0, ROWS // TILE), jax.random.fold_in(arg_keys[5], 1), 0, (ROWS // TILE) - 1).astype(jnp.int32)
    tile_counts = draw_tile_counts(jax.random.fold_in(arg_keys[8], 71), 0)
    cotangent = draw_cotangent(jax.random.fold_in(arg_keys[8], 71), 0)
    return {"features": features, "weight": weight, "bias": bias, "tile_values": tile_values, "tile_rows": tile_rows, "tile_cols": tile_cols, "tile_counts": tile_counts, "cotangent": cotangent}


def activate(values):
    return jax.nn.gelu(values, approximate=True)

def tile_places(tile_rows, tile_cols, tile_counts):
    devices_all = N_LOOP * N_REP
    slot_total = N_LOOP * KB
    row_tiles = ROWS // TILE
    device_ids = jnp.arange(devices_all, dtype=jnp.int32)
    loop_of = device_ids // N_REP
    rep_of = device_ids % N_REP
    slot_ids = jnp.arange(slot_total, dtype=jnp.int32)
    block_of = slot_ids // KB
    shifted = tile_rows // row_tiles - BAND
    near_block = (rep_of[:, None] + shifted) % N_REP
    row_place = ((loop_of[:, None] * N_REP + near_block) * row_tiles + tile_rows % row_tiles).astype(jnp.int32)
    column_place = ((block_of[None, :] * N_REP + rep_of[:, None]) * row_tiles + tile_cols).astype(jnp.int32)
    live_mask = ((slot_ids % KB)[None, :] < jnp.repeat(tile_counts, KB, axis=1)).astype(jnp.float32)
    return (row_place, column_place, live_mask)

def spread_tiles(tile_values, take_index, put_index, live_mask, field, flipped):
    tiles_all = NODES // TILE
    field_tiles = field.reshape(tiles_all, TILE, H)
    slot_total = N_LOOP * KB
    values_by_loop = tile_values.reshape(N_LOOP, N_REP, slot_total, TILE, TILE)
    take_by_loop = take_index.reshape(N_LOOP, N_REP, slot_total)
    put_by_loop = put_index.reshape(N_LOOP, N_REP, slot_total)
    live_by_loop = live_mask.reshape(N_LOOP, N_REP, slot_total)
    einsum_form = 'rsba,rsbh->rsah' if flipped else 'rsab,rsbh->rsah'

    def one_block(accum, inputs):
        block_values, block_take, block_put, block_live = inputs
        chosen = field_tiles[block_take]
        product = jnp.einsum(einsum_form, block_values, chosen, precision=lax.Precision.HIGHEST)
        product = product * block_live[:, :, None, None]
        return (accum.at[block_put].add(product), None)
    start_value = jnp.zeros((tiles_all, TILE, H), jnp.float32)
    result = lax.scan(one_block, start_value, (values_by_loop, take_by_loop, put_by_loop, live_by_loop))[0]
    return result.reshape(NODES, H)

def reference(features, weight, bias, tile_values, tile_rows, tile_cols, tile_counts, cotangent):
    row_place, column_place, live_mask = tile_places(tile_rows, tile_cols, tile_counts)
    gathered = spread_tiles(tile_values, column_place, row_place, live_mask, features, False)
    pre_act = jnp.dot(gathered, weight, precision=lax.Precision.HIGHEST, preferred_element_type=jnp.float32) + bias
    output, pull_back = jax.vjp(activate, pre_act)
    grad_pre = pull_back(cotangent)[0]
    grad_agg = jnp.dot(grad_pre, weight.T, precision=lax.Precision.HIGHEST, preferred_element_type=jnp.float32)
    grad_features = spread_tiles(tile_values, row_place, column_place, live_mask, grad_agg, True)
    grad_weight = jnp.dot(gathered.T, grad_pre, precision=lax.Precision.HIGHEST, preferred_element_type=jnp.float32) / NODES
    grad_bias = lax.optimization_barrier(jnp.sum(grad_pre, axis=0)) / NODES
    return (output, grad_features, grad_weight, grad_bias)
```

```python
import functools

import jax
import jax.numpy as jnp
from jax import lax
from jax.experimental import pallas as pl
from jax.experimental.pallas import tpu as pltpu
from jax.sharding import Mesh
from jax.sharding import PartitionSpec as P

Z_HI, CORE, X, Y, Z_LO = 4, 2, 4, 8, 3
AXES = ("z_hi", "core", "x", "y", "z_lo")
LOOP = ("z_hi", "core")
REP = ("x", "y", "z_lo")
N_REP = X * Y * Z_LO
COLUMN_BLOCKS = Z_HI * CORE
PER_BLOCK = 4
TILE = 128
ROWS = 256
H = 256
NODES = 196608
VMEM_LIMIT = 48 * 1024 * 1024

BAND_PLACE = ((3, 4, 0, 1, 2), (3, 2, 0, 1, 4), (1, 2, 0, 3, 4))


def split(value):
    high = value.astype(jnp.bfloat16)
    low = (value - high.astype(jnp.float32)).astype(jnp.bfloat16)
    return high, low


def dot(left, right):
    return jnp.dot(left, right, preferred_element_type=jnp.float32)


def dot3(left_high, left_low, right_high, right_low):
    return dot(left_high, right_high) + (dot(left_low, right_high) + dot(left_high, right_low))


def params():
    return pltpu.CompilerParams(vmem_limit_bytes=VMEM_LIMIT)


def cost(flops, size):
    return pl.CostEstimate(flops=flops, bytes_accessed=size, transcendentals=0)


def place_kernel(cols, counts, tiles, high, low, high_t, low_t):
    block = pl.program_id(0)
    for slot in range(PER_BLOCK):
        live = slot < counts[block]
        column = cols[block * PER_BLOCK + slot]
        tile = jnp.where(live, tiles[slot], 0.0)
        tile_t = tile.T
        span = pl.ds(slot * TILE, TILE)
        for half in range(ROWS // TILE):
            half_span = pl.ds(half * TILE, TILE)
            placed_high, placed_low = split(jnp.where(column == half, tile, 0.0))
            high[0, span, half_span] = placed_high
            low[0, span, half_span] = placed_low
            placed_high, placed_low = split(jnp.where(column == half, tile_t, 0.0))
            high_t[0, half_span, span] = placed_high
            low_t[0, half_span, span] = placed_low


def place_tiles(tiles, cols, counts):
    deep = PER_BLOCK * TILE
    plain = jax.ShapeDtypeStruct((COLUMN_BLOCKS, deep, ROWS), jnp.bfloat16)
    turned = jax.ShapeDtypeStruct((COLUMN_BLOCKS, ROWS, deep), jnp.bfloat16)
    plain_spec = pl.BlockSpec((1, deep, ROWS), lambda i, *_: (i, 0, 0))
    turned_spec = pl.BlockSpec((1, ROWS, deep), lambda i, *_: (i, 0, 0))
    return pl.pallas_call(
        place_kernel,
        grid_spec=pltpu.PrefetchScalarGridSpec(
            num_scalar_prefetch=2,
            grid=(COLUMN_BLOCKS,),
            in_specs=[pl.BlockSpec((PER_BLOCK, TILE, TILE), lambda i, *_: (i, 0, 0))],
            out_specs=[plain_spec, plain_spec, turned_spec, turned_spec],
        ),
        out_shape=[plain, plain, turned, turned],
        compiler_params=params(),
        cost_estimate=cost(0, 10 << 20),
        name="place_tiles",
    )(cols, counts, tiles)


def gather_kernel(n, carried, ids, rows, high, low, *refs):
    fields = refs[:n]
    before = refs[n : n + carried]
    outs = refs[n + carried : -1]
    total = refs[-1]
    step = pl.program_id(0)

    @pl.when(step == 0)
    def _():
        for j in range(5):
            total[2 * j : 2 * j + 2] = (
                before[j][...].reshape(2, TILE, H) if carried else jnp.zeros((2, TILE, H), jnp.float32)
            )

    for j in range(n):

        @pl.when(step == j)
        def _(j=j):
            field_high, field_low = split(fields[j][...])
            product = dot3(high[0], low[0], field_high, field_low)
            for slot in range(PER_BLOCK):
                row = rows[ids[j] * PER_BLOCK + slot]
                total[row] += product[slot * TILE : (slot + 1) * TILE]

    @pl.when(step == n - 1)
    def _():
        for j in range(5):
            outs[j][...] = total[2 * j : 2 * j + 2].reshape(ROWS, H)


def gather_terms(ids, rows, high, low, fields, before=()):
    n = len(fields)
    whole = pl.BlockSpec((ROWS, H), lambda i, *_: (0, 0))
    tiles = pl.BlockSpec((1, PER_BLOCK * TILE, ROWS), lambda i, ids, rows: (ids[i], 0, 0))
    return pl.pallas_call(
        functools.partial(gather_kernel, n, len(before)),
        grid_spec=pltpu.PrefetchScalarGridSpec(
            num_scalar_prefetch=2,
            grid=(n,),
            in_specs=[tiles, tiles] + [whole] * (n + len(before)),
            out_specs=[whole] * 5,
            scratch_shapes=[pltpu.VMEM((10, TILE, H), jnp.float32)],
        ),
        out_shape=[jax.ShapeDtypeStruct((ROWS, H), jnp.float32)] * 5,
        compiler_params=params(),
        cost_estimate=cost(n * 6 * 512 * 256 * 256, n << 20),
        name="gather_terms",
    )(ids, rows, high, low, *fields, *before)


def dense_kernel(own, from_a, from_b, weight, bias, cotangent, agg, output, grad_pre, grad_agg):
    total = own[...] + from_a[...] + from_b[...]
    agg[...] = total
    weight_high, weight_low = split(weight[...])
    value = dot3(*split(total), weight_high, weight_low) + bias[...]
    scale = 0.7978845608028654
    square = value * value
    turn = jnp.tanh(scale * (value + 0.044715 * (square * value)))
    half = 0.5 * (1.0 + turn)
    output[...] = value * half
    slope = half + 0.5 * value * (1.0 - turn * turn) * (scale * (1.0 + 3.0 * 0.044715 * square))
    grad = cotangent[...] * slope
    grad_pre[...] = grad
    turned_high, turned_low = split(weight[...].T)
    grad_agg[...] = dot3(*split(grad), turned_high, turned_low)


def dense(own, from_a, from_b, weight, bias, cotangent):
    return pl.pallas_call(
        dense_kernel,
        out_shape=[jax.ShapeDtypeStruct((ROWS, H), jnp.float32)] * 4,
        compiler_params=params(),
        cost_estimate=cost(12 * 256 * 256 * 256, 10 * 256 * 1024),
        name="dense",
    )(own, from_a, from_b, weight, bias.reshape(1, H), cotangent)


def weight_kernel(agg, grad_pre, weight_term, bias_term):
    weight_term[...] = dot3(*split(agg[...].T), *split(grad_pre[...]))
    bias_term[...] = jnp.sum(grad_pre[...], axis=0, keepdims=True)


def weight_terms(agg, grad_pre):
    return pl.pallas_call(
        weight_kernel,
        out_shape=[
            jax.ShapeDtypeStruct((H, H), jnp.float32),
            jax.ShapeDtypeStruct((1, H), jnp.float32),
        ],
        compiler_params=params(),
        cost_estimate=cost(6 * 256 * 256 * 256, 3 * 256 * 1024),
        name="weight_terms",
    )(agg, grad_pre)


def spread_kernel(ids, rows, high_t, low_t, own, a, b, y1, y2, out, band_high, band_low):
    step = pl.program_id(0)

    @pl.when(step == 0)
    def _():
        for j, ref in enumerate((own, a, b, y1, y2)):
            high, low = split(ref[...])
            band_high[2 * j : 2 * j + 2] = high.reshape(2, TILE, H)
            band_low[2 * j : 2 * j + 2] = low.reshape(2, TILE, H)

    first = ids[step] * PER_BLOCK
    places = [rows[first + slot] for slot in range(PER_BLOCK)]
    chosen_high = jnp.concatenate([band_high[place] for place in places], axis=0)
    chosen_low = jnp.concatenate([band_low[place] for place in places], axis=0)
    out[0] = dot3(high_t[0], low_t[0], chosen_high, chosen_low)


def spread_terms(ids, rows, high_t, low_t, band):
    n = ids.shape[0]
    whole = pl.BlockSpec((ROWS, H), lambda i, *_: (0, 0))
    tiles = pl.BlockSpec((1, ROWS, PER_BLOCK * TILE), lambda i, ids, rows: (ids[i], 0, 0))
    return pl.pallas_call(
        spread_kernel,
        grid_spec=pltpu.PrefetchScalarGridSpec(
            num_scalar_prefetch=2,
            grid=(n,),
            in_specs=[tiles, tiles] + [whole] * 5,
            out_specs=pl.BlockSpec((1, ROWS, H), lambda i, *_: (i, 0, 0)),
            scratch_shapes=[pltpu.VMEM((10, TILE, H), jnp.bfloat16)] * 2,
        ),
        out_shape=jax.ShapeDtypeStruct((n, ROWS, H), jnp.float32),
        compiler_params=params(),
        cost_estimate=cost(n * 6 * 512 * 256 * 256, n << 20),
        name="spread_terms",
    )(ids, rows, high_t, low_t, *band)


def other_core(value):
    return lax.ppermute(value, "core", [(0, 1), (1, 0)])


def along_loop(value, sign):
    pairs = []
    for z in range(Z_HI):
        for core in range(CORE):
            by = sign if core == 0 else -sign
            pairs.append((z * CORE + core, (z + by) % Z_HI * CORE + core))
    return lax.ppermute(value, LOOP, pairs)


def in_triple(value, by):
    return lax.ppermute(value, "z_lo", [(i, (i + by) % Z_LO) for i in range(Z_LO)])


def across_triples(value, by):
    pairs = [(r, (r + Z_LO * by[r % Z_LO]) % N_REP) for r in range(N_REP)]
    return lax.ppermute(value, REP, pairs)


def whole_sums(weight_term, bias_term):
    plane = ("x", "y")
    column = ("z_hi", "core", "z_lo")
    n_plane, n_column = X * Y, Z_HI * CORE * Z_LO
    rows = H // n_plane
    part = lax.all_to_all(weight_term.reshape(n_plane, rows, H), plane, 0, 0, tiled=True)
    part = jnp.sum(part, axis=0)
    part = jnp.concatenate([part, jnp.pad(bias_term.reshape(rows, H // rows), ((0, 0), (0, 128 - H // rows)))], axis=1)
    part = lax.all_to_all(
        jnp.broadcast_to(part[None], (n_column,) + part.shape), column, 0, 0, tiled=True
    )
    part = jnp.sum(part, axis=0)
    part = lax.all_to_all(jnp.broadcast_to(part[None], (n_plane,) + part.shape), plane, 0, 0, tiled=True)
    weight_whole = part[:, :, :H].reshape(H, H)
    bias_whole = jnp.sum(part[:, :, H : H + H // rows], axis=0).reshape(H)
    return weight_whole, bias_whole


def per_device(features, weight, bias, tile_values, tile_rows, tile_cols, tile_counts, cotangent):
    z_hi, core, z_lo = lax.axis_index("z_hi"), lax.axis_index("core"), lax.axis_index("z_lo")
    places = jnp.asarray(BAND_PLACE, jnp.int32)[z_lo]
    row_tiles = ROWS // TILE
    rows = jnp.take(places, tile_rows[0] // row_tiles) * row_tiles + tile_rows[0] % row_tiles
    cols = tile_cols[0]
    counts = tile_counts[0]

    turn = 1 - 2 * core
    first = (z_hi - turn) % Z_HI
    second = (z_hi + turn) % Z_HI
    far = (z_hi + 2) % Z_HI

    def block(z, c):
        return z * CORE + c

    field_first = along_loop(features, 1)
    field_second = along_loop(features, -1)
    field_other = other_core(features)
    high, low, high_t, low_t = place_tiles(tile_values[0], cols, counts)
    field_far = along_loop(field_first, 1)
    other_first = other_core(field_first)
    other_second = other_core(field_second)
    near_ids = jnp.stack(
        [
            block(z_hi, core),
            block(z_hi, 1 - core),
            block(first, core),
            block(second, 1 - core),
            block(second, core),
            block(first, 1 - core),
        ]
    )
    terms = gather_terms(
        near_ids,
        rows,
        high,
        low,
        (features, field_other, field_first, other_first, field_second, other_second),
    )
    other_far = other_core(field_far)
    far_ids = jnp.stack([block(far, core), block(far, 1 - core)])
    own, term_a, term_b, term_y1, term_y2 = gather_terms(
        far_ids, rows, high, low, (field_far, other_far), terms
    )

    got_y1 = across_triples(term_y1, (-1, -1, 1))
    got_y2 = across_triples(term_y2, (-1, 1, 1))
    got_a = in_triple(term_a + got_y1, 1)
    got_b = in_triple(term_b + got_y2, 2)
    agg, output, grad_pre, grad_agg = dense(own, got_a, got_b, weight, bias, cotangent)

    band_a = in_triple(grad_agg, -1)
    band_b = in_triple(grad_agg, -2)
    weight_term, bias_term = weight_terms(agg, grad_pre)
    band_y1 = across_triples(band_a, (1, 1, -1))
    band_y2 = across_triples(band_b, (1, -1, -1))
    band = (grad_agg, band_a, band_b, band_y1, band_y2)

    other_ids = jnp.stack(
        [block(far, 1 - core), block(second, 1 - core), block(first, 1 - core), block(z_hi, 1 - core)]
    )
    own_ids = jnp.stack([block(far, core), block(first, core), block(second, core), block(z_hi, core)])
    given = other_core(spread_terms(other_ids, rows, high_t, low_t, band))
    kept = spread_terms(own_ids, rows, high_t, low_t, band)
    got_far = along_loop(kept[0] + given[0], -1)
    got_second = along_loop(kept[2] + given[2], 1)
    got_first = along_loop(kept[1] + given[1] + got_far, -1)
    grad_features = kept[3] + given[3] + got_first + got_second

    weight_whole, bias_whole = whole_sums(weight_term, bias_term)
    return (output, grad_features, weight_whole / NODES, bias_whole / NODES)


def solution(mesh):
    cut = Mesh(mesh.devices.reshape(Z_HI, CORE, X, Y, Z_LO), AXES)
    nodes = P(AXES)
    return jax.shard_map(
        per_device,
        mesh=cut,
        in_specs=(nodes, P(), P(), nodes, nodes, nodes, nodes, nodes),
        out_specs=(nodes, nodes, P(), P()),
        check_vma=False,
    )
```

```python
import functools

import jax
import jax.numpy as jnp
from jax import lax
from jax.experimental import pallas as pl
from jax.experimental.pallas import tpu as pltpu
from jax.sharding import Mesh
from jax.sharding import PartitionSpec as P

Z_HI, CORE, X, Y, Z_LO = 4, 2, 4, 8, 3
AXES = ("z_hi", "core", "x", "y", "z_lo")
LOOP = ("z_hi", "core")
REP = ("x", "y", "z_lo")
N_REP = X * Y * Z_LO
COLUMN_BLOCKS = Z_HI * CORE
PER_BLOCK = 4
TILE = 128
ROWS = 256
H = 256
NODES = 196608
PLANE = ("x", "y")
COLUMN = ("z_hi", "core", "z_lo")
N_PLANE = X * Y
N_COLUMN = Z_HI * CORE * Z_LO
PART = 256 // N_PLANE
VMEM_LIMIT = 16 * 1024 * 1024

BAND_PLACE = ((3, 4, 0, 1, 2), (3, 2, 0, 1, 4), (1, 2, 0, 3, 4))


def split(value):
    high = value.astype(jnp.bfloat16)
    low = (value - high.astype(jnp.float32)).astype(jnp.bfloat16)
    return high, low


def dot(left, right):
    return jnp.dot(left, right, preferred_element_type=jnp.float32)


def dot3(left_high, left_low, right_high, right_low):
    return dot(left_high, right_high) + (dot(left_low, right_high) + dot(left_high, right_low))


def in_hbm(value):
    return pltpu.with_memory_space_constraint(value, pltpu.HBM)


def params():
    return pltpu.CompilerParams(vmem_limit_bytes=VMEM_LIMIT)


LONG = pl.CostEstimate(flops=1 << 40, bytes_accessed=1 << 32, transcendentals=1 << 30)
SHORT = pl.CostEstimate(flops=1 << 10, bytes_accessed=1 << 10, transcendentals=0)


def cost(flops, size):
    return pl.CostEstimate(flops=flops, bytes_accessed=size, transcendentals=0)


def place_kernel(info, tiles, high, low):
    block = pl.program_id(0)
    for slot in range(PER_BLOCK):
        column, live = column_and_live(info, block, slot)
        tile = jnp.where(live, tiles[slot], 0.0).T
        span = pl.ds(slot * TILE, TILE)
        for half in range(ROWS // TILE):
            half_span = pl.ds(half * TILE, TILE)
            high[0, half_span, span], low[0, half_span, span] = split(jnp.where(column == half, tile, 0.0))


def place_tiles(info, tiles):
    shape = (ROWS, PER_BLOCK * TILE)
    spec = pl.BlockSpec((1,) + shape, lambda i, *_: (i, 0, 0))
    return pl.pallas_call(
        place_kernel,
        grid_spec=pltpu.PrefetchScalarGridSpec(
            num_scalar_prefetch=1,
            grid=(COLUMN_BLOCKS,),
            in_specs=[pl.BlockSpec((PER_BLOCK, TILE, TILE), lambda i, *_: (i, 0, 0))],
            out_specs=[spec, spec],
        ),
        out_shape=[pltpu.HBM((COLUMN_BLOCKS,) + shape, jnp.bfloat16)] * 2,
        compiler_params=params(),
        cost_estimate=cost(0, 6 << 20),
        name="place_tiles",
    )(info, in_hbm(tiles))


GATHER_NEAR, GATHER_MIDDLE, GATHER_FAR, SPREAD_OTHER, SPREAD_OWN = 0, 3, 6, 8, 12
PLACES_AT = 16
ROWS_AT = PLACES_AT + 5
COLS_AT = ROWS_AT + COLUMN_BLOCKS * PER_BLOCK
COUNTS_AT = COLS_AT + COLUMN_BLOCKS * PER_BLOCK


def band_row(info, block, slot):
    row = info[ROWS_AT + block * PER_BLOCK + slot]
    return info[PLACES_AT + (row >> 1)] * 2 + (row & 1)


def column_and_live(info, block, slot):
    return info[COLS_AT + block * PER_BLOCK + slot], slot < info[COUNTS_AT + block]


def gather_kernel(n, carried, at, info, tiles, *refs):
    fields = refs[:n]
    before = refs[n : n + carried]
    outs = refs[n + carried : -1]
    total = refs[-1]
    step = pl.program_id(0)

    @pl.when(step == 0)
    def _():
        for j in range(5):
            total[2 * j : 2 * j + 2] = (
                before[j][...].reshape(2, TILE, H) if carried else jnp.zeros((2, TILE, H), jnp.float32)
            )

    for j in range(n):

        @pl.when(step == j)
        def _(j=j):
            block = info[at + j]
            field_high, field_low = split(fields[j][...])
            placed = []
            for slot in range(PER_BLOCK):
                column, live = column_and_live(info, block, slot)
                tile = jnp.where(live, tiles[slot], 0.0)
                halves = [jnp.where(column == half, tile, 0.0) for half in range(ROWS // TILE)]
                placed.append(jnp.concatenate(halves, axis=1))
            high, low = split(jnp.concatenate(placed, axis=0))
            product = dot3(high, low, field_high, field_low)
            for slot in range(PER_BLOCK):
                row = band_row(info, block, slot)
                total[row] += product[slot * TILE : (slot + 1) * TILE]

    @pl.when(step == n - 1)
    def _():
        for j in range(5):
            outs[j][...] = total[2 * j : 2 * j + 2].reshape(ROWS, H)


def gather_terms(at, info, tiles, fields, before=()):
    n = len(fields)
    whole = pl.BlockSpec((ROWS, H), lambda i, *_: (0, 0))
    block = pl.BlockSpec((PER_BLOCK, TILE, TILE), lambda i, info: (info[at + i], 0, 0))
    return pl.pallas_call(
        functools.partial(gather_kernel, n, len(before), at),
        grid_spec=pltpu.PrefetchScalarGridSpec(
            num_scalar_prefetch=1,
            grid=(n,),
            in_specs=[block] + [whole] * (n + len(before)),
            out_specs=[whole] * 5,
            scratch_shapes=[pltpu.VMEM((10, TILE, H), jnp.float32)],
        ),
        out_shape=[jax.ShapeDtypeStruct((ROWS, H), jnp.float32)] * 5,
        compiler_params=params(),
        cost_estimate=SHORT,
        name="gather_terms",
    )(info, in_hbm(tiles), *fields, *before)


def dense_kernel(own, *refs):
    got, (weight, bias, cotangent, agg, output, grad_pre, grad_agg) = refs[:-7], refs[-7:]
    total = own[...]
    for ref in got:
        total += ref[...]
    agg[...] = total
    weight_high, weight_low = split(weight[...])
    value = dot3(*split(total), weight_high, weight_low) + bias[...]
    scale = 0.7978845608028654
    square = value * value
    turn = jnp.tanh(scale * (value + 0.044715 * (square * value)))
    half = 0.5 * (1.0 + turn)
    output[...] = value * half
    slope = half + 0.5 * value * (1.0 - turn * turn) * (scale * (1.0 + 3.0 * 0.044715 * square))
    grad = cotangent[...] * slope
    grad_pre[...] = grad
    turned_high, turned_low = split(weight[...].T)
    grad_agg[...] = dot3(*split(grad), turned_high, turned_low)


def dense(own, got, weight, bias, cotangent):
    return pl.pallas_call(
        dense_kernel,
        out_shape=[jax.ShapeDtypeStruct((ROWS, H), jnp.float32)] * 4,
        compiler_params=params(),
        cost_estimate=cost(12 * 256 * 256 * 256, 10 * 256 * 1024),
        name="dense",
    )(own, *got, weight, bias.reshape(1, H), cotangent)


def weight_kernel(agg, grad_pre, weight_term, bias_term):
    weight_term[...] = dot3(*split(agg[...].T), *split(grad_pre[...]))
    total = jnp.sum(grad_pre[...], axis=0, keepdims=True)
    wide = H // PART
    bias_term[...] = jnp.zeros_like(bias_term)
    for j in range(PART):
        bias_term[j : j + 1, :wide] = total[:, j * wide : (j + 1) * wide]


def weight_terms(agg, grad_pre):
    return pl.pallas_call(
        weight_kernel,
        out_shape=[
            pltpu.HBM((H, H), jnp.float32),
            pltpu.HBM((PART, 128), jnp.float32),
        ],
        compiler_params=params(),
        cost_estimate=cost(6 * 256 * 256 * 256, 3 * 256 * 1024),
        name="weight_terms",
    )(agg, grad_pre)


def spread_kernel(at, info, high_t, low_t, own, a, b, y1, y2, *refs):
    outs, (band_high, band_low) = refs[:-2], refs[-2:]
    step = pl.program_id(0)

    @pl.when(step == 0)
    def _():
        for j, ref in enumerate((own, a, b, y1, y2)):
            high, low = split(ref[...])
            band_high[2 * j : 2 * j + 2] = high.reshape(2, TILE, H)
            band_low[2 * j : 2 * j + 2] = low.reshape(2, TILE, H)

    block = info[at + step]
    chosen = [band_row(info, block, slot) for slot in range(PER_BLOCK)]
    chosen_high = jnp.concatenate([band_high[row] for row in chosen], axis=0)
    chosen_low = jnp.concatenate([band_low[row] for row in chosen], axis=0)
    product = dot3(high_t[0], low_t[0], chosen_high, chosen_low)
    if len(outs) == 1:
        outs[0][0] = product
    else:
        for j, out in enumerate(outs):

            @pl.when(step == j)
            def _(out=out):
                out[...] = product


def spread_terms(at, n, info, high_t, low_t, band, apart=False):
    whole = pl.BlockSpec((ROWS, H), lambda i, *_: (0, 0))
    tiles = pl.BlockSpec((1, ROWS, PER_BLOCK * TILE), lambda i, info: (info[at + i], 0, 0))
    return pl.pallas_call(
        functools.partial(spread_kernel, at),
        grid_spec=pltpu.PrefetchScalarGridSpec(
            num_scalar_prefetch=1,
            grid=(n,),
            in_specs=[tiles, tiles] + [whole] * 5,
            out_specs=[whole] * n if apart else pl.BlockSpec((1, ROWS, H), lambda i, *_: (i, 0, 0)),
            scratch_shapes=[pltpu.VMEM((10, TILE, H), jnp.bfloat16)] * 2,
        ),
        out_shape=[pltpu.HBM((ROWS, H), jnp.float32)] * n if apart else pltpu.HBM((n, ROWS, H), jnp.float32),
        compiler_params=params(),
        cost_estimate=LONG,
        name="spread_terms",
    )(info, in_hbm(high_t), in_hbm(low_t), *band)


def turn_kernel(kept_first, given_first, far, kept, given, second, passed, held):
    passed[...] = kept_first[...] + given_first[0] + far[...]
    held[...] = kept[...] + given[0] + second[...]


def turn_terms(kept_first, kept, given, far, second):
    whole = pl.BlockSpec((ROWS, H), lambda i: (0, 0))
    return pl.pallas_call(
        turn_kernel,
        grid=(1,),
        in_specs=[
            whole,
            pl.BlockSpec((1, ROWS, H), lambda i: (1, 0, 0)),
            whole,
            whole,
            pl.BlockSpec((1, ROWS, H), lambda i: (3, 0, 0)),
            whole,
        ],
        out_specs=[whole, whole],
        out_shape=[jax.ShapeDtypeStruct((ROWS, H), jnp.float32)] * 2,
        compiler_params=params(),
        cost_estimate=LONG,
        name="turn_terms",
    )(kept_first, given, far, kept, given, second)


def other_core(value):
    return lax.ppermute(value, "core", [(0, 1), (1, 0)])


def along_loop(value, sign):
    pairs = []
    for z in range(Z_HI):
        for core in range(CORE):
            by = sign if core == 0 else -sign
            pairs.append((z * CORE + core, (z + by) % Z_HI * CORE + core))
    return lax.ppermute(value, LOOP, pairs)


def in_triple(value, by):
    return lax.ppermute(value, "z_lo", [(i, (i + by) % Z_LO) for i in range(Z_LO)])


def across_triples(value, by):
    pairs = [(r, (r + Z_LO * by[r % Z_LO]) % N_REP) for r in range(N_REP)]
    return lax.ppermute(value, REP, pairs)


def swap(value, axes):
    return lax.all_to_all(value, axes, 0, 0, tiled=True)


def copy_kernel(parts, bias_part, out):
    total = jnp.sum(parts[...], axis=0)
    if bias_part is not None:
        total = jnp.concatenate([total, bias_part[...]], axis=1)
    for j in range(out.shape[0]):
        out[j] = total


def sum_and_copy(parts, copies, bias_part=None):
    width = parts.shape[2] + (0 if bias_part is None else bias_part.shape[1])
    if bias_part is None:
        kernel = lambda parts, out: copy_kernel(parts, None, out)
    else:
        kernel = copy_kernel
    return pl.pallas_call(
        kernel,
        out_shape=jax.ShapeDtypeStruct((copies, PART, width), jnp.float32),
        compiler_params=params(),
        cost_estimate=cost(1 << 10, 1 << 10),
        name="sum_and_copy",
    )(*((parts,) if bias_part is None else (parts, bias_part)))


def read_kernel(whole, weight_whole, bias_whole):
    for j in range(N_PLANE):
        weight_whole[j * PART : (j + 1) * PART, :] = whole[j, :, :H] / NODES
    bias_part = jnp.sum(whole[:, :, H:], axis=0) / NODES
    wide = H // PART
    for j in range(PART):
        bias_whole[:, j * wide : (j + 1) * wide] = bias_part[j : j + 1, :wide]


def read_sums(whole):
    weight_whole, bias_whole = pl.pallas_call(
        read_kernel,
        out_shape=[jax.ShapeDtypeStruct((H, H), jnp.float32), jax.ShapeDtypeStruct((1, H), jnp.float32)],
        compiler_params=params(),
        name="read_sums",
    )(whole)
    return weight_whole, bias_whole.reshape(H)


def after(value, *others):
    return lax.optimization_barrier((value,) + others)


def per_device(features, weight, bias, tile_values, tile_rows, tile_cols, tile_counts, cotangent):
    z_hi, core, z_lo = lax.axis_index("z_hi"), lax.axis_index("core"), lax.axis_index("z_lo")

    turn = 1 - 2 * core
    first = (z_hi - turn) % Z_HI
    second = (z_hi + turn) % Z_HI
    far = (z_hi + 2) % Z_HI

    def block(z, c):
        return z * CORE + c

    blocks = [
        block(z_hi, core),
        block(z_hi, 1 - core),
        block(first, core),
        block(second, 1 - core),
        block(second, core),
        block(first, 1 - core),
        block(far, core),
        block(far, 1 - core),
        block(far, 1 - core),
        block(second, 1 - core),
        block(first, 1 - core),
        block(z_hi, 1 - core),
        block(far, core),
        block(first, core),
        block(second, core),
        block(z_hi, core),
    ]
    places = [
        jnp.where(z_lo == 0, line[0], jnp.where(z_lo == 1, line[1], line[2])) for line in zip(*BAND_PLACE)
    ]
    (scalars,) = after(jnp.stack(blocks + places))
    info = jnp.concatenate([scalars, tile_rows[0], tile_cols[0], tile_counts[0]])

    first_upper = along_loop(features[:TILE], 1)
    first_lower = along_loop(features[TILE:], 1)
    field_second = along_loop(features, -1)
    field_other = other_core(features)
    first_upper, info = after(first_upper, info)
    far_upper = along_loop(first_upper, 1)
    far_lower = along_loop(first_lower, 1)
    field_first = jnp.concatenate([first_upper, first_lower])
    field_far = jnp.concatenate([far_upper, far_lower])
    other_first = other_core(field_first)
    terms = gather_terms(GATHER_NEAR, info, tile_values[0], (features, field_other, field_first))
    far_upper, field_second, *terms = after(far_upper, field_second, *terms)
    other_second = other_core(field_second)
    other_far = other_core(field_far)
    terms = gather_terms(GATHER_MIDDLE, info, tile_values[0], (other_first, field_second, other_second), terms)
    own, term_a, term_b, term_y1, term_y2 = gather_terms(
        GATHER_FAR, info, tile_values[0], (field_far, other_far), terms
    )

    high_t, low_t = place_tiles(info, tile_values[0])
    got_y1 = across_triples(term_y1, (-1, -1, 1))
    got_y2 = across_triples(term_y2, (-1, 1, 1))
    got_a = in_triple(term_a + got_y1, 1)
    got_b = in_triple(term_b + got_y2, 2)
    got_a, got_b, high_t, low_t = after(got_a, got_b, high_t, low_t)
    agg, output, grad_pre, grad_agg = dense(own, (got_a, got_b), weight, bias, cotangent)
    band_a = in_triple(grad_agg, -1)
    band_b = in_triple(grad_agg, -2)
    weight_term, bias_term = weight_terms(agg, grad_pre)
    band_a, band_b, _ = after(band_a, band_b, weight_term)
    band_y1 = across_triples(band_a, (1, 1, -1))
    band_y2 = across_triples(band_b, (1, -1, -1))
    sums = swap(weight_term.reshape(N_PLANE, PART, H), PLANE)
    sums = sum_and_copy(sums, N_COLUMN, bias_term)
    band = (grad_agg, band_a, band_b, band_y1, band_y2)
    sums = sum_and_copy(swap(sums, COLUMN), N_PLANE)

    given = other_core(spread_terms(SPREAD_OTHER, 4, info, high_t, low_t, band))
    kept_far, kept_first, kept_second, kept = spread_terms(SPREAD_OWN, 4, info, high_t, low_t, band, apart=True)
    got_far = along_loop(kept_far + given[0], -1)
    got_second = along_loop(kept_second + given[2], 1)
    passed, held = turn_terms(kept_first, kept, given, got_far, got_second)
    grad_features = held + along_loop(passed, -1)
    weight_whole, bias_whole = read_sums(swap(sums, PLANE))
    return (output, grad_features, weight_whole, bias_whole)


def solution(mesh):
    cut = Mesh(mesh.devices.reshape(Z_HI, CORE, X, Y, Z_LO), AXES)
    nodes = P(AXES)
    return jax.shard_map(
        per_device,
        mesh=cut,
        in_specs=(nodes, P(), P(), nodes, nodes, nodes, nodes, nodes),
        out_specs=(nodes, nodes, P(), P()),
        check_vma=False,
    )
```

```python
import functools

import jax
import jax.numpy as jnp
from jax import lax
from jax.experimental import pallas as pl
from jax.experimental.pallas import tpu as pltpu
from jax.sharding import Mesh
from jax.sharding import PartitionSpec as P

Z_HI, CORE, X, Y, Z_LO = 4, 2, 4, 8, 3
AXES = ("z_hi", "core", "x", "y", "z_lo")
LOOP = ("z_hi", "core")
REP = ("x", "y", "z_lo")
N_REP = X * Y * Z_LO
COLUMN_BLOCKS = Z_HI * CORE
PER_BLOCK = 4
TILE = 128
ROWS = 256
H = 256
NODES = 196608
PLANE = ("x", "y")
COLUMN = ("z_hi", "core", "z_lo")
N_PLANE = X * Y
N_COLUMN = Z_HI * CORE * Z_LO
PART = 256 // N_PLANE
VMEM_LIMIT = 20 * 1024 * 1024

BAND_PLACE = ((3, 4, 0, 1, 2), (3, 2, 0, 1, 4), (1, 2, 0, 3, 4))


def split(value):
    high = value.astype(jnp.bfloat16)
    low = (value - high.astype(jnp.float32)).astype(jnp.bfloat16)
    return high, low


def dot(left, right):
    return jnp.dot(left, right, preferred_element_type=jnp.float32)


def dot3(left_high, left_low, right_high, right_low):
    return dot(left_high, right_high) + (dot(left_low, right_high) + dot(left_high, right_low))


def in_hbm(value):
    return pltpu.with_memory_space_constraint(value, pltpu.HBM)


def params():
    return pltpu.CompilerParams(vmem_limit_bytes=VMEM_LIMIT)


LONG = pl.CostEstimate(flops=1 << 40, bytes_accessed=1 << 32, transcendentals=1 << 30)
SHORT = pl.CostEstimate(flops=1 << 10, bytes_accessed=1 << 10, transcendentals=0)


def cost(flops, size):
    return pl.CostEstimate(flops=flops, bytes_accessed=size, transcendentals=0)


def place_kernel(info, tiles, high, low):
    block = pl.program_id(0)
    for slot in range(PER_BLOCK):
        column, live = column_and_live(info, block, slot)
        tile = jnp.where(live, tiles[slot], 0.0).T
        span = pl.ds(slot * TILE, TILE)
        for half in range(ROWS // TILE):
            half_span = pl.ds(half * TILE, TILE)
            high[0, half_span, span], low[0, half_span, span] = split(jnp.where(column == half, tile, 0.0))


def place_tiles(info, tiles):
    shape = (ROWS, PER_BLOCK * TILE)
    spec = pl.BlockSpec((1,) + shape, lambda i, *_: (i, 0, 0))
    return pl.pallas_call(
        place_kernel,
        grid_spec=pltpu.PrefetchScalarGridSpec(
            num_scalar_prefetch=1,
            grid=(COLUMN_BLOCKS,),
            in_specs=[pl.BlockSpec((PER_BLOCK, TILE, TILE), lambda i, *_: (i, 0, 0))],
            out_specs=[spec, spec],
        ),
        out_shape=[pltpu.HBM((COLUMN_BLOCKS,) + shape, jnp.bfloat16)] * 2,
        compiler_params=params(),
        cost_estimate=cost(0, 6 << 20),
        name="place_tiles",
    )(info, in_hbm(tiles))


GATHER_NEAR, GATHER_MIDDLE, GATHER_FAR, SPREAD_OTHER, SPREAD_OWN = 0, 3, 6, 8, 12
PLACES_AT = 16
ROWS_AT = PLACES_AT + 5
COLS_AT = ROWS_AT + COLUMN_BLOCKS * PER_BLOCK
COUNTS_AT = COLS_AT + COLUMN_BLOCKS * PER_BLOCK


def band_row(info, block, slot):
    row = info[ROWS_AT + block * PER_BLOCK + slot]
    return info[PLACES_AT + (row >> 1)] * 2 + (row & 1)


def column_and_live(info, block, slot):
    return info[COLS_AT + block * PER_BLOCK + slot], slot < info[COUNTS_AT + block]


def gather_kernel(n, carried, at, info, *refs):
    tiles, fields = refs[:n], refs[n : 2 * n]
    before = refs[2 * n : 2 * n + carried]
    outs, total = refs[2 * n + carried : -1], refs[-1]
    for j in range(5):
        total[2 * j : 2 * j + 2] = (
            before[j][...].reshape(2, TILE, H) if carried else jnp.zeros((2, TILE, H), jnp.float32)
        )
    for j in range(n):
        block = info[at + j]
        field_high, field_low = split(fields[j][...])
        placed = []
        for slot in range(PER_BLOCK):
            column, live = column_and_live(info, block, slot)
            tile = jnp.where(live, tiles[j][slot], 0.0)
            halves = [jnp.where(column == half, tile, 0.0) for half in range(ROWS // TILE)]
            placed.append(jnp.concatenate(halves, axis=1))
        high, low = split(jnp.concatenate(placed, axis=0))
        product = dot3(high, low, field_high, field_low)
        for slot in range(PER_BLOCK):
            row = band_row(info, block, slot)
            total[row] += product[slot * TILE : (slot + 1) * TILE]
    for j in range(5):
        outs[j][...] = total[2 * j : 2 * j + 2].reshape(ROWS, H)


def gather_terms(at, info, tiles, fields, before=()):
    n = len(fields)
    whole = pl.BlockSpec((ROWS, H), lambda i, *_: (0, 0))
    blocks = [
        pl.BlockSpec((PER_BLOCK, TILE, TILE), lambda i, info, j=j: (info[at + j], 0, 0)) for j in range(n)
    ]
    return pl.pallas_call(
        functools.partial(gather_kernel, n, len(before), at),
        grid_spec=pltpu.PrefetchScalarGridSpec(
            num_scalar_prefetch=1,
            grid=(1,),
            in_specs=blocks + [whole] * (n + len(before)),
            out_specs=[whole] * 5,
            scratch_shapes=[pltpu.VMEM((10, TILE, H), jnp.float32)],
        ),
        out_shape=[jax.ShapeDtypeStruct((ROWS, H), jnp.float32)] * 5,
        compiler_params=params(),
        cost_estimate=SHORT,
        name="gather_terms",
    )(info, *([in_hbm(tiles)] * n), *fields, *before)


def dense_kernel(own, *refs):
    got, (weight, bias, cotangent, agg, output, grad_pre, grad_agg) = refs[:-7], refs[-7:]
    total = own[...]
    for ref in got:
        total += ref[...]
    agg[...] = total
    weight_high, weight_low = split(weight[...])
    value = dot3(*split(total), weight_high, weight_low) + bias[...]
    scale = 0.7978845608028654
    square = value * value
    turn = jnp.tanh(scale * (value + 0.044715 * (square * value)))
    half = 0.5 * (1.0 + turn)
    output[...] = value * half
    slope = half + 0.5 * value * (1.0 - turn * turn) * (scale * (1.0 + 3.0 * 0.044715 * square))
    grad = cotangent[...] * slope
    grad_pre[...] = grad
    turned_high, turned_low = split(weight[...].T)
    grad_agg[...] = dot3(*split(grad), turned_high, turned_low)


def dense(own, got, weight, bias, cotangent):
    return pl.pallas_call(
        dense_kernel,
        out_shape=[jax.ShapeDtypeStruct((ROWS, H), jnp.float32)] * 4,
        compiler_params=params(),
        cost_estimate=cost(12 * 256 * 256 * 256, 10 * 256 * 1024),
        name="dense",
    )(own, *got, weight, bias.reshape(1, H), cotangent)


def weight_kernel(agg, grad_pre, weight_term, bias_term):
    weight_term[...] = dot3(*split(agg[...].T), *split(grad_pre[...]))
    total = jnp.sum(grad_pre[...], axis=0, keepdims=True)
    wide = H // PART
    bias_term[...] = jnp.zeros_like(bias_term)
    for j in range(PART):
        bias_term[j : j + 1, :wide] = total[:, j * wide : (j + 1) * wide]


def weight_terms(agg, grad_pre):
    return pl.pallas_call(
        weight_kernel,
        out_shape=[
            pltpu.HBM((H, H), jnp.float32),
            pltpu.HBM((PART, 128), jnp.float32),
        ],
        compiler_params=params(),
        cost_estimate=cost(6 * 256 * 256 * 256, 3 * 256 * 1024),
        name="weight_terms",
    )(agg, grad_pre)


def spread_kernel(at, n, info, *refs):
    highs, lows = refs[:n], refs[n : 2 * n]
    band, outs, (band_high, band_low) = refs[2 * n : 2 * n + 5], refs[2 * n + 5 : -2], refs[-2:]
    for j, ref in enumerate(band):
        high, low = split(ref[...])
        band_high[2 * j : 2 * j + 2] = high.reshape(2, TILE, H)
        band_low[2 * j : 2 * j + 2] = low.reshape(2, TILE, H)
    for j in range(n):
        chosen = [band_row(info, info[at + j], slot) for slot in range(PER_BLOCK)]
        chosen_high = jnp.concatenate([band_high[row] for row in chosen], axis=0)
        chosen_low = jnp.concatenate([band_low[row] for row in chosen], axis=0)
        product = dot3(highs[j][0], lows[j][0], chosen_high, chosen_low)
        if len(outs) == 1:
            outs[0][j] = product
        else:
            outs[j][...] = product


def spread_terms(at, n, info, high_t, low_t, band, apart=False):
    whole = pl.BlockSpec((ROWS, H), lambda i, *_: (0, 0))
    tiles = [
        pl.BlockSpec((1, ROWS, PER_BLOCK * TILE), lambda i, info, j=j: (info[at + j], 0, 0)) for j in range(n)
    ]
    return pl.pallas_call(
        functools.partial(spread_kernel, at, n),
        grid_spec=pltpu.PrefetchScalarGridSpec(
            num_scalar_prefetch=1,
            grid=(1,),
            in_specs=tiles * 2 + [whole] * 5,
            out_specs=[whole] * n if apart else pl.BlockSpec((n, ROWS, H), lambda i, *_: (0, 0, 0)),
            scratch_shapes=[pltpu.VMEM((10, TILE, H), jnp.bfloat16)] * 2,
        ),
        out_shape=[pltpu.HBM((ROWS, H), jnp.float32)] * n if apart else pltpu.HBM((n, ROWS, H), jnp.float32),
        compiler_params=params(),
        cost_estimate=LONG,
        name="spread_terms",
    )(info, *([in_hbm(high_t)] * n), *([in_hbm(low_t)] * n), *band)


def turn_kernel(kept_first, given_first, far, kept, given, second, passed, held):
    passed[...] = kept_first[...] + given_first[0] + far[...]
    held[...] = kept[...] + given[0] + second[...]


def turn_terms(kept_first, kept, given, far, second):
    whole = pl.BlockSpec((ROWS, H), lambda i: (0, 0))
    return pl.pallas_call(
        turn_kernel,
        grid=(1,),
        in_specs=[
            whole,
            pl.BlockSpec((1, ROWS, H), lambda i: (1, 0, 0)),
            whole,
            whole,
            pl.BlockSpec((1, ROWS, H), lambda i: (3, 0, 0)),
            whole,
        ],
        out_specs=[whole, whole],
        out_shape=[jax.ShapeDtypeStruct((ROWS, H), jnp.float32)] * 2,
        compiler_params=params(),
        cost_estimate=LONG,
        name="turn_terms",
    )(kept_first, given, far, kept, given, second)


def other_core(value):
    return lax.ppermute(value, "core", [(0, 1), (1, 0)])


def along_loop(value, sign):
    pairs = []
    for z in range(Z_HI):
        for core in range(CORE):
            by = sign if core == 0 else -sign
            pairs.append((z * CORE + core, (z + by) % Z_HI * CORE + core))
    return lax.ppermute(value, LOOP, pairs)


def in_triple(value, by):
    return lax.ppermute(value, "z_lo", [(i, (i + by) % Z_LO) for i in range(Z_LO)])


def across_triples(value, by):
    pairs = [(r, (r + Z_LO * by[r % Z_LO]) % N_REP) for r in range(N_REP)]
    return lax.ppermute(value, REP, pairs)


def swap(value, axes):
    return lax.all_to_all(value, axes, 0, 0, tiled=True)


def copy_kernel(parts, bias_part, out):
    total = jnp.sum(parts[...], axis=0)
    if bias_part is not None:
        total = jnp.concatenate([total, bias_part[...]], axis=1)
    for j in range(out.shape[0]):
        out[j] = total


def sum_and_copy(parts, copies, bias_part=None):
    width = parts.shape[2] + (0 if bias_part is None else bias_part.shape[1])
    if bias_part is None:
        kernel = lambda parts, out: copy_kernel(parts, None, out)
    else:
        kernel = copy_kernel
    return pl.pallas_call(
        kernel,
        out_shape=jax.ShapeDtypeStruct((copies, PART, width), jnp.float32),
        compiler_params=params(),
        cost_estimate=cost(1 << 10, 1 << 10),
        name="sum_and_copy",
    )(*((parts,) if bias_part is None else (parts, bias_part)))


def read_kernel(whole, weight_whole, bias_whole):
    for j in range(N_PLANE):
        weight_whole[j * PART : (j + 1) * PART, :] = whole[j, :, :H] / NODES
    bias_part = jnp.sum(whole[:, :, H:], axis=0) / NODES
    wide = H // PART
    for j in range(PART):
        bias_whole[:, j * wide : (j + 1) * wide] = bias_part[j : j + 1, :wide]


def read_sums(whole):
    weight_whole, bias_whole = pl.pallas_call(
        read_kernel,
        out_shape=[jax.ShapeDtypeStruct((H, H), jnp.float32), jax.ShapeDtypeStruct((1, H), jnp.float32)],
        compiler_params=params(),
        name="read_sums",
    )(whole)
    return weight_whole, bias_whole.reshape(H)


def after(value, *others):
    return lax.optimization_barrier((value,) + others)


def per_device(features, weight, bias, tile_values, tile_rows, tile_cols, tile_counts, cotangent):
    z_hi, core, z_lo = lax.axis_index("z_hi"), lax.axis_index("core"), lax.axis_index("z_lo")

    turn = 1 - 2 * core
    first = (z_hi - turn) % Z_HI
    second = (z_hi + turn) % Z_HI
    far = (z_hi + 2) % Z_HI

    def block(z, c):
        return z * CORE + c

    blocks = [
        block(z_hi, core),
        block(z_hi, 1 - core),
        block(first, core),
        block(second, 1 - core),
        block(second, core),
        block(first, 1 - core),
        block(far, core),
        block(far, 1 - core),
        block(far, 1 - core),
        block(second, 1 - core),
        block(first, 1 - core),
        block(z_hi, 1 - core),
        block(far, core),
        block(first, core),
        block(second, core),
        block(z_hi, core),
    ]
    places = [
        jnp.where(z_lo == 0, line[0], jnp.where(z_lo == 1, line[1], line[2])) for line in zip(*BAND_PLACE)
    ]
    (scalars,) = after(jnp.stack(blocks + places))
    info = jnp.concatenate([scalars, tile_rows[0], tile_cols[0], tile_counts[0]])

    first_upper = along_loop(features[:TILE], 1)
    first_lower = along_loop(features[TILE:], 1)
    field_second = along_loop(features, -1)
    first_upper, own_field, info = after(first_upper, features, info)
    field_other = other_core(own_field)
    far_upper = along_loop(first_upper, 1)
    far_lower = along_loop(first_lower, 1)
    field_first = jnp.concatenate([first_upper, first_lower])
    field_far = jnp.concatenate([far_upper, far_lower])
    other_first = other_core(field_first)
    terms = gather_terms(GATHER_NEAR, info, tile_values[0], (features, field_other, field_first))
    far_upper, field_second, *terms = after(far_upper, field_second, *terms)
    other_second = other_core(field_second)
    other_far = other_core(field_far)
    terms = gather_terms(GATHER_MIDDLE, info, tile_values[0], (other_first, field_second, other_second), terms)
    own, term_a, term_b, term_y1, term_y2 = gather_terms(
        GATHER_FAR, info, tile_values[0], (field_far, other_far), terms
    )

    high_t, low_t = place_tiles(info, tile_values[0])
    got_y1 = across_triples(term_y1, (-1, -1, 1))
    got_y2 = across_triples(term_y2, (-1, 1, 1))
    got_a = in_triple(term_a + got_y1, 1)
    got_b = in_triple(term_b + got_y2, 2)
    got_a, got_b, high_t, low_t = after(got_a, got_b, high_t, low_t)
    agg, output, grad_pre, grad_agg = dense(own, (got_a, got_b), weight, bias, cotangent)
    band_a = in_triple(grad_agg, -1)
    band_b = in_triple(grad_agg, -2)
    weight_term, bias_term = weight_terms(agg, grad_pre)
    band_a, band_b, _ = after(band_a, band_b, weight_term)
    band_y1 = across_triples(band_a, (1, 1, -1))
    band_y2 = across_triples(band_b, (1, -1, -1))
    sums = swap(weight_term.reshape(N_PLANE, PART, H), PLANE)
    sums = sum_and_copy(sums, N_COLUMN, bias_term)
    band = (grad_agg, band_a, band_b, band_y1, band_y2)
    sums = sum_and_copy(swap(sums, COLUMN), N_PLANE)

    given = other_core(spread_terms(SPREAD_OTHER, 4, info, high_t, low_t, band))
    kept_far, kept_first, kept_second, kept = spread_terms(SPREAD_OWN, 4, info, high_t, low_t, band, apart=True)
    got_far = along_loop(kept_far + given[0], -1)
    got_second = along_loop(kept_second + given[2], 1)
    passed, held = turn_terms(kept_first, kept, given, got_far, got_second)
    weight_whole, bias_whole = read_sums(swap(sums, PLANE))
    held, weight_whole, bias_whole = after(held, weight_whole, bias_whole)
    grad_features = held + along_loop(passed, -1)
    return (output, grad_features, weight_whole, bias_whole)


def solution(mesh):
    cut = Mesh(mesh.devices.reshape(Z_HI, CORE, X, Y, Z_LO), AXES)
    nodes = P(AXES)
    return jax.shard_map(
        per_device,
        mesh=cut,
        in_specs=(nodes, P(), P(), nodes, nodes, nodes, nodes, nodes),
        out_specs=(nodes, nodes, P(), P()),
        check_vma=False,
    )
```

```python
import functools

import jax
import jax.numpy as jnp
from jax import lax
from jax.experimental import pallas as pl
from jax.experimental.pallas import tpu as pltpu
from jax.sharding import Mesh
from jax.sharding import PartitionSpec as P

Z_HI, CORE, X, Y, Z_LO = 4, 2, 4, 8, 3
AXES = ("z_hi", "core", "x", "y", "z_lo")
LOOP = ("z_hi", "core")
REP = ("x", "y", "z_lo")
N_REP = X * Y * Z_LO
COLUMN_BLOCKS = Z_HI * CORE
PER_BLOCK = 4
TILE = 128
PLACED = 2
ROWS = 256
H = 256
NODES = 196608
PLANE = ("x", "y")
COLUMN = ("z_hi", "core", "z_lo")
N_PLANE = X * Y
N_COLUMN = Z_HI * CORE * Z_LO
PART = 256 // N_PLANE
VMEM_LIMIT = 20 * 1024 * 1024

BAND_PLACE = ((3, 4, 0, 1, 2), (3, 2, 0, 1, 4), (1, 2, 0, 3, 4))


def split(value):
    high = value.astype(jnp.bfloat16)
    low = (value - high.astype(jnp.float32)).astype(jnp.bfloat16)
    return high, low


def dot(left, right):
    return jnp.dot(left, right, preferred_element_type=jnp.float32)


def dot3(left_high, left_low, right_high, right_low):
    return dot(left_high, right_high) + (dot(left_low, right_high) + dot(left_high, right_low))


def in_hbm(value):
    return pltpu.with_memory_space_constraint(value, pltpu.HBM)


def params():
    return pltpu.CompilerParams(vmem_limit_bytes=VMEM_LIMIT)


LONG = pl.CostEstimate(flops=1 << 40, bytes_accessed=1 << 32, transcendentals=1 << 30)
SHORT = pl.CostEstimate(flops=1 << 10, bytes_accessed=1 << 10, transcendentals=0)


def cost(flops, size):
    return pl.CostEstimate(flops=flops, bytes_accessed=size, transcendentals=0)


def place_kernel(info, tiles, high, low):
    for j in range(PLACED):
        block = pl.program_id(0) * PLACED + j
        for slot in range(PER_BLOCK):
            column, live = column_and_live(info, block, slot)
            tile = jnp.where(live, tiles[j * PER_BLOCK + slot], 0.0).T
            span = pl.ds(slot * TILE, TILE)
            for half in range(ROWS // TILE):
                half_span = pl.ds(half * TILE, TILE)
                high[j, half_span, span], low[j, half_span, span] = split(jnp.where(column == half, tile, 0.0))


def place_tiles(info, tiles):
    shape = (ROWS, PER_BLOCK * TILE)
    spec = pl.BlockSpec((PLACED,) + shape, lambda i, *_: (i, 0, 0))
    return pl.pallas_call(
        place_kernel,
        grid_spec=pltpu.PrefetchScalarGridSpec(
            num_scalar_prefetch=1,
            grid=(COLUMN_BLOCKS // PLACED,),
            in_specs=[pl.BlockSpec((PLACED * PER_BLOCK, TILE, TILE), lambda i, *_: (i, 0, 0))],
            out_specs=[spec, spec],
        ),
        out_shape=[pltpu.HBM((COLUMN_BLOCKS,) + shape, jnp.bfloat16)] * 2,
        compiler_params=params(),
        cost_estimate=cost(0, 6 << 20),
        name="place_tiles",
    )(info, in_hbm(tiles))


GATHER_NEAR, GATHER_MIDDLE, GATHER_FAR, SPREAD_OTHER, SPREAD_OWN = 0, 3, 6, 8, 12
PLACES_AT = 16
ROWS_AT = PLACES_AT + 5
COLS_AT = ROWS_AT + COLUMN_BLOCKS * PER_BLOCK
COUNTS_AT = COLS_AT + COLUMN_BLOCKS * PER_BLOCK


def band_row(info, block, slot):
    row = info[ROWS_AT + block * PER_BLOCK + slot]
    return info[PLACES_AT + (row >> 1)] * 2 + (row & 1)


def column_and_live(info, block, slot):
    return info[COLS_AT + block * PER_BLOCK + slot], slot < info[COUNTS_AT + block]


def gather_kernel(n, carried, at, info, *refs):
    tiles, fields = refs[:n], refs[n : 2 * n]
    before = refs[2 * n : 2 * n + carried]
    outs, total = refs[2 * n + carried : -1], refs[-1]
    for j in range(5):
        total[2 * j : 2 * j + 2] = (
            before[j][...].reshape(2, TILE, H) if carried else jnp.zeros((2, TILE, H), jnp.float32)
        )
    for j in range(n):
        block = info[at + j]
        field_high, field_low = split(fields[j][...])
        placed = []
        for slot in range(PER_BLOCK):
            column, live = column_and_live(info, block, slot)
            tile = jnp.where(live, tiles[j][slot], 0.0)
            halves = [jnp.where(column == half, tile, 0.0) for half in range(ROWS // TILE)]
            placed.append(jnp.concatenate(halves, axis=1))
        high, low = split(jnp.concatenate(placed, axis=0))
        product = dot3(high, low, field_high, field_low)
        for slot in range(PER_BLOCK):
            row = band_row(info, block, slot)
            total[row] += product[slot * TILE : (slot + 1) * TILE]
    for j in range(5):
        outs[j][...] = total[2 * j : 2 * j + 2].reshape(ROWS, H)


def gather_terms(at, info, tiles, fields, before=()):
    n = len(fields)
    whole = pl.BlockSpec((ROWS, H), lambda i, *_: (0, 0))
    blocks = [
        pl.BlockSpec((PER_BLOCK, TILE, TILE), lambda i, info, j=j: (info[at + j], 0, 0)) for j in range(n)
    ]
    return pl.pallas_call(
        functools.partial(gather_kernel, n, len(before), at),
        grid_spec=pltpu.PrefetchScalarGridSpec(
            num_scalar_prefetch=1,
            grid=(1,),
            in_specs=blocks + [whole] * (n + len(before)),
            out_specs=[whole] * 5,
            scratch_shapes=[pltpu.VMEM((10, TILE, H), jnp.float32)],
        ),
        out_shape=[jax.ShapeDtypeStruct((ROWS, H), jnp.float32)] * 5,
        compiler_params=params(),
        cost_estimate=SHORT,
        name="gather_terms",
    )(info, *([in_hbm(tiles)] * n), *fields, *before)


def dense_kernel(own, *refs):
    got, (weight, bias, cotangent, agg, output, grad_pre, grad_agg) = refs[:-7], refs[-7:]
    total = own[...]
    for ref in got:
        total += ref[...]
    agg[...] = total
    weight_high, weight_low = split(weight[...])
    value = dot3(*split(total), weight_high, weight_low) + bias[...]
    scale = 0.7978845608028654
    square = value * value
    turn = jnp.tanh(scale * (value + 0.044715 * (square * value)))
    half = 0.5 * (1.0 + turn)
    output[...] = value * half
    slope = half + 0.5 * value * (1.0 - turn * turn) * (scale * (1.0 + 3.0 * 0.044715 * square))
    grad = cotangent[...] * slope
    grad_pre[...] = grad
    turned_high, turned_low = split(weight[...].T)
    grad_agg[...] = dot3(*split(grad), turned_high, turned_low)


def dense(own, got, weight, bias, cotangent):
    return pl.pallas_call(
        dense_kernel,
        out_shape=[jax.ShapeDtypeStruct((ROWS, H), jnp.float32)] * 4,
        compiler_params=params(),
        cost_estimate=cost(12 * 256 * 256 * 256, 10 * 256 * 1024),
        name="dense",
    )(own, *got, weight, bias.reshape(1, H), cotangent)


def weight_kernel(agg, grad_pre, weight_term, bias_term):
    weight_term[...] = dot3(*split(agg[...].T), *split(grad_pre[...]))
    total = jnp.sum(grad_pre[...], axis=0, keepdims=True)
    wide = H // PART
    bias_term[...] = jnp.zeros_like(bias_term)
    for j in range(PART):
        bias_term[j : j + 1, :wide] = total[:, j * wide : (j + 1) * wide]


def weight_terms(agg, grad_pre):
    return pl.pallas_call(
        weight_kernel,
        out_shape=[
            pltpu.HBM((H, H), jnp.float32),
            jax.ShapeDtypeStruct((PART, 128), jnp.float32),
        ],
        compiler_params=params(),
        cost_estimate=cost(6 * 256 * 256 * 256, 3 * 256 * 1024),
        name="weight_terms",
    )(agg, grad_pre)


def spread_kernel(at, n, info, *refs):
    highs, lows = refs[:n], refs[n : 2 * n]
    band, outs, (band_high, band_low) = refs[2 * n : 2 * n + 5], refs[2 * n + 5 : -2], refs[-2:]
    for j, ref in enumerate(band):
        high, low = split(ref[...])
        band_high[2 * j : 2 * j + 2] = high.reshape(2, TILE, H)
        band_low[2 * j : 2 * j + 2] = low.reshape(2, TILE, H)
    for j in range(n):
        chosen = [band_row(info, info[at + j], slot) for slot in range(PER_BLOCK)]
        chosen_high = jnp.concatenate([band_high[row] for row in chosen], axis=0)
        chosen_low = jnp.concatenate([band_low[row] for row in chosen], axis=0)
        product = dot3(highs[j][0], lows[j][0], chosen_high, chosen_low)
        if len(outs) == 1:
            outs[0][j] = product
        else:
            outs[j][...] = product


def spread_terms(at, n, info, high_t, low_t, band, apart=False):
    whole = pl.BlockSpec((ROWS, H), lambda i, *_: (0, 0))
    tiles = [
        pl.BlockSpec((1, ROWS, PER_BLOCK * TILE), lambda i, info, j=j: (info[at + j], 0, 0)) for j in range(n)
    ]
    return pl.pallas_call(
        functools.partial(spread_kernel, at, n),
        grid_spec=pltpu.PrefetchScalarGridSpec(
            num_scalar_prefetch=1,
            grid=(1,),
            in_specs=tiles * 2 + [whole] * 5,
            out_specs=[whole] * n if apart else pl.BlockSpec((n, ROWS, H), lambda i, *_: (0, 0, 0)),
            scratch_shapes=[pltpu.VMEM((10, TILE, H), jnp.bfloat16)] * 2,
        ),
        out_shape=[pltpu.HBM((ROWS, H), jnp.float32)] * n if apart else pltpu.HBM((n, ROWS, H), jnp.float32),
        compiler_params=params(),
        cost_estimate=LONG,
        name="spread_terms",
    )(info, *([in_hbm(high_t)] * n), *([in_hbm(low_t)] * n), *band)


def turn_kernel(kept_first, given_first, far, kept, given, second, passed, held):
    passed[...] = kept_first[...] + given_first[0] + far[...]
    held[...] = kept[...] + given[0] + second[...]


def turn_terms(kept_first, kept, given, far, second):
    whole = pl.BlockSpec((ROWS, H), lambda i: (0, 0))
    return pl.pallas_call(
        turn_kernel,
        grid=(1,),
        in_specs=[
            whole,
            pl.BlockSpec((1, ROWS, H), lambda i: (1, 0, 0)),
            whole,
            whole,
            pl.BlockSpec((1, ROWS, H), lambda i: (3, 0, 0)),
            whole,
        ],
        out_specs=[whole, whole],
        out_shape=[jax.ShapeDtypeStruct((ROWS, H), jnp.float32)] * 2,
        compiler_params=params(),
        cost_estimate=LONG,
        name="turn_terms",
    )(kept_first, given, far, kept, given, second)


def other_core(value):
    return lax.ppermute(value, "core", [(0, 1), (1, 0)])


def along_loop(value, sign):
    pairs = []
    for z in range(Z_HI):
        for core in range(CORE):
            by = sign if core == 0 else -sign
            pairs.append((z * CORE + core, (z + by) % Z_HI * CORE + core))
    return lax.ppermute(value, LOOP, pairs)


def in_triple(value, by):
    return lax.ppermute(value, "z_lo", [(i, (i + by) % Z_LO) for i in range(Z_LO)])


def across_triples(value, by):
    pairs = [(r, (r + Z_LO * by[r % Z_LO]) % N_REP) for r in range(N_REP)]
    return lax.ppermute(value, REP, pairs)


def swap(value, axes):
    return lax.all_to_all(value, axes, 0, 0, tiled=True)


def copy_kernel(parts, bias_part, out):
    total = jnp.sum(parts[...], axis=0)
    if bias_part is not None:
        total = jnp.concatenate([total, bias_part[...]], axis=1)
    for j in range(out.shape[0]):
        out[j] = total


def sum_and_copy(parts, copies, bias_part=None):
    width = parts.shape[2] + (0 if bias_part is None else bias_part.shape[1])
    if bias_part is None:
        kernel = lambda parts, out: copy_kernel(parts, None, out)
    else:
        kernel = copy_kernel
    return pl.pallas_call(
        kernel,
        out_shape=jax.ShapeDtypeStruct((copies, PART, width), jnp.float32),
        compiler_params=params(),
        cost_estimate=cost(1 << 10, 1 << 10),
        name="sum_and_copy",
    )(*((parts,) if bias_part is None else (parts, bias_part)))


def read_kernel(whole, weight_whole, bias_whole):
    for j in range(N_PLANE):
        weight_whole[j * PART : (j + 1) * PART, :] = whole[j, :, :H] / NODES
    bias_part = jnp.sum(whole[:, :, H:], axis=0) / NODES
    wide = H // PART
    for j in range(PART):
        bias_whole[:, j * wide : (j + 1) * wide] = bias_part[j : j + 1, :wide]


def read_sums(whole):
    weight_whole, bias_whole = pl.pallas_call(
        read_kernel,
        out_shape=[jax.ShapeDtypeStruct((H, H), jnp.float32), jax.ShapeDtypeStruct((1, H), jnp.float32)],
        compiler_params=params(),
        name="read_sums",
    )(whole)
    return weight_whole, bias_whole.reshape(H)


def after(value, *others):
    return lax.optimization_barrier((value,) + others)


def per_device(features, weight, bias, tile_values, tile_rows, tile_cols, tile_counts, cotangent):
    z_hi, core, z_lo = lax.axis_index("z_hi"), lax.axis_index("core"), lax.axis_index("z_lo")

    turn = 1 - 2 * core
    first = (z_hi - turn) % Z_HI
    second = (z_hi + turn) % Z_HI
    far = (z_hi + 2) % Z_HI

    def block(z, c):
        return z * CORE + c

    blocks = [
        block(z_hi, core),
        block(z_hi, 1 - core),
        block(first, core),
        block(second, 1 - core),
        block(second, core),
        block(first, 1 - core),
        block(far, core),
        block(far, 1 - core),
        block(far, 1 - core),
        block(second, 1 - core),
        block(first, 1 - core),
        block(z_hi, 1 - core),
        block(far, core),
        block(first, core),
        block(second, core),
        block(z_hi, core),
    ]
    places = [
        jnp.where(z_lo == 0, line[0], jnp.where(z_lo == 1, line[1], line[2])) for line in zip(*BAND_PLACE)
    ]
    (scalars,) = after(jnp.stack(blocks + places))
    info = jnp.concatenate([scalars, tile_rows[0], tile_cols[0], tile_counts[0]])

    first_upper = along_loop(features[:TILE], 1)
    first_lower = along_loop(features[TILE:], 1)
    field_second = along_loop(features, -1)
    first_upper, own_field, info = after(first_upper, features, info)
    field_other = other_core(own_field)
    far_upper = along_loop(first_upper, 1)
    far_lower = along_loop(first_lower, 1)
    field_first = jnp.concatenate([first_upper, first_lower])
    field_far = jnp.concatenate([far_upper, far_lower])
    other_first = other_core(field_first)
    terms = gather_terms(GATHER_NEAR, info, tile_values[0], (in_hbm(features), field_other, field_first))
    far_upper, field_second, *terms = after(far_upper, field_second, *terms)
    other_second = other_core(field_second)
    other_far = other_core(field_far)
    terms = gather_terms(GATHER_MIDDLE, info, tile_values[0], (other_first, field_second, other_second), terms)
    own, term_a, term_b, term_y1, term_y2 = gather_terms(
        GATHER_FAR, info, tile_values[0], (field_far, other_far), terms
    )

    high_t, low_t = place_tiles(info, tile_values[0])
    got_y1 = across_triples(term_y1, (-1, -1, 1))
    got_y2 = across_triples(term_y2, (-1, 1, 1))
    got_a = in_triple(term_a + got_y1, 1)
    got_b = in_triple(term_b + got_y2, 2)
    got_a, got_b, high_t, low_t = after(got_a, got_b, high_t, low_t)
    agg, output, grad_pre, grad_agg = dense(own, (got_a, got_b), weight, bias, cotangent)
    band_a = in_triple(grad_agg, -1)
    band_b = in_triple(grad_agg, -2)
    weight_term, bias_term = weight_terms(agg, grad_pre)
    band_a, band_b, _ = after(band_a, band_b, weight_term)
    band_y1 = across_triples(band_a, (1, 1, -1))
    band_y2 = across_triples(band_b, (1, -1, -1))
    sums = swap(weight_term.reshape(N_PLANE, PART, H), PLANE)
    sums = sum_and_copy(sums, N_COLUMN, bias_term)
    band = (grad_agg, band_a, band_b, band_y1, band_y2)
    sums = sum_and_copy(swap(sums, COLUMN), N_PLANE)

    given = other_core(spread_terms(SPREAD_OTHER, 4, info, high_t, low_t, band))
    kept_far, kept_first, kept_second, kept = spread_terms(SPREAD_OWN, 4, info, high_t, low_t, band, apart=True)
    got_far = along_loop(kept_far + given[0], -1)
    got_second = along_loop(kept_second + given[2], 1)
    passed, held = turn_terms(kept_first, kept, given, got_far, got_second)
    weight_whole, bias_whole = read_sums(swap(sums, PLANE))
    held, weight_whole, bias_whole = after(held, weight_whole, bias_whole)
    grad_features = held + along_loop(passed, -1)
    return (output, grad_features, weight_whole, bias_whole)


def solution(mesh):
    cut = Mesh(mesh.devices.reshape(Z_HI, CORE, X, Y, Z_LO), AXES)
    nodes = P(AXES)
    return jax.shard_map(
        per_device,
        mesh=cut,
        in_specs=(nodes, P(), P(), nodes, nodes, nodes, nodes, nodes),
        out_specs=(nodes, nodes, P(), P()),
        check_vma=False,
    )
```

```python
import functools

import jax
import jax.numpy as jnp
from jax import lax
from jax.experimental import pallas as pl
from jax.experimental.pallas import tpu as pltpu
from jax.sharding import Mesh
from jax.sharding import PartitionSpec as P

Z_HI, CORE, X, Y, Z_LO = 4, 2, 4, 8, 3
AXES = ("z_hi", "core", "x", "y", "z_lo")
LOOP = ("z_hi", "core")
REP = ("x", "y", "z_lo")
N_REP = X * Y * Z_LO
COLUMN_BLOCKS = Z_HI * CORE
PER_BLOCK = 4
TILE = 128
PLACED = 2
ROWS = 256
H = 256
NODES = 196608
PLANE = ("x", "y")
COLUMN = ("z_hi", "core", "z_lo")
N_PLANE = X * Y
N_COLUMN = Z_HI * CORE * Z_LO
PART = 256 // N_PLANE
VMEM_LIMIT = 20 * 1024 * 1024

BAND_PLACE = ((3, 4, 0, 1, 2), (3, 2, 0, 1, 4), (1, 2, 0, 3, 4))


def split(value):
    high = value.astype(jnp.bfloat16)
    low = (value - high.astype(jnp.float32)).astype(jnp.bfloat16)
    return high, low


def dot(left, right):
    return jnp.dot(left, right, preferred_element_type=jnp.float32)


def dot3(left_high, left_low, right_high, right_low):
    return dot(left_high, right_high) + (dot(left_low, right_high) + dot(left_high, right_low))


def in_hbm(value):
    return pltpu.with_memory_space_constraint(value, pltpu.HBM)


def params():
    return pltpu.CompilerParams(vmem_limit_bytes=VMEM_LIMIT)


LONG = pl.CostEstimate(flops=1 << 40, bytes_accessed=1 << 32, transcendentals=1 << 30)
SHORT = pl.CostEstimate(flops=1 << 10, bytes_accessed=1 << 10, transcendentals=0)


def cost(flops, size):
    return pl.CostEstimate(flops=flops, bytes_accessed=size, transcendentals=0)


def place_kernel(info, tiles, high, low):
    for j in range(PLACED):
        block = pl.program_id(0) * PLACED + j
        for slot in range(PER_BLOCK):
            column, live = column_and_live(info, block, slot)
            tile = jnp.where(live, tiles[j * PER_BLOCK + slot], 0.0).T
            span = pl.ds(slot * TILE, TILE)
            for half in range(ROWS // TILE):
                half_span = pl.ds(half * TILE, TILE)
                high[j, half_span, span], low[j, half_span, span] = split(jnp.where(column == half, tile, 0.0))


def place_tiles(info, tiles):
    shape = (ROWS, PER_BLOCK * TILE)
    spec = pl.BlockSpec((PLACED,) + shape, lambda i, *_: (i, 0, 0))
    return pl.pallas_call(
        place_kernel,
        grid_spec=pltpu.PrefetchScalarGridSpec(
            num_scalar_prefetch=1,
            grid=(COLUMN_BLOCKS // PLACED,),
            in_specs=[pl.BlockSpec((PLACED * PER_BLOCK, TILE, TILE), lambda i, *_: (i, 0, 0))],
            out_specs=[spec, spec],
        ),
        out_shape=[pltpu.HBM((COLUMN_BLOCKS,) + shape, jnp.bfloat16)] * 2,
        compiler_params=params(),
        cost_estimate=cost(0, 6 << 20),
        name="place_tiles",
    )(info, in_hbm(tiles))


GATHER_NEAR, GATHER_MIDDLE, GATHER_FAR, SPREAD_OTHER, SPREAD_OWN = 0, 3, 6, 8, 12
PLACES_AT = 16
ROWS_AT = PLACES_AT + 5
COLS_AT = ROWS_AT + COLUMN_BLOCKS * PER_BLOCK
COUNTS_AT = COLS_AT + COLUMN_BLOCKS * PER_BLOCK


def band_row(info, block, slot):
    row = info[ROWS_AT + block * PER_BLOCK + slot]
    return info[PLACES_AT + (row >> 1)] * 2 + (row & 1)


def column_and_live(info, block, slot):
    return info[COLS_AT + block * PER_BLOCK + slot], slot < info[COUNTS_AT + block]


def gather_kernel(n, carried, at, info, *refs):
    tiles, fields = refs[:n], refs[n : 2 * n]
    before = refs[2 * n : 2 * n + carried]
    outs, total = refs[2 * n + carried : -1], refs[-1]
    for j in range(5):
        total[2 * j : 2 * j + 2] = (
            before[j][...].reshape(2, TILE, H) if carried else jnp.zeros((2, TILE, H), jnp.float32)
        )
    for j in range(n):
        block = info[at + j]
        field_high, field_low = split(fields[j][...])
        placed = []
        for slot in range(PER_BLOCK):
            column, live = column_and_live(info, block, slot)
            tile = jnp.where(live, tiles[j][slot], 0.0)
            halves = [jnp.where(column == half, tile, 0.0) for half in range(ROWS // TILE)]
            placed.append(jnp.concatenate(halves, axis=1))
        high, low = split(jnp.concatenate(placed, axis=0))
        product = dot3(high, low, field_high, field_low)
        for slot in range(PER_BLOCK):
            row = band_row(info, block, slot)
            total[row] += product[slot * TILE : (slot + 1) * TILE]
    for j in range(5):
        outs[j][...] = total[2 * j : 2 * j + 2].reshape(ROWS, H)


def gather_terms(at, info, tiles, fields, before=()):
    n = len(fields)
    whole = pl.BlockSpec((ROWS, H), lambda i, *_: (0, 0))
    blocks = [
        pl.BlockSpec((PER_BLOCK, TILE, TILE), lambda i, info, j=j: (info[at + j], 0, 0)) for j in range(n)
    ]
    return pl.pallas_call(
        functools.partial(gather_kernel, n, len(before), at),
        grid_spec=pltpu.PrefetchScalarGridSpec(
            num_scalar_prefetch=1,
            grid=(1,),
            in_specs=blocks + [whole] * (n + len(before)),
            out_specs=[whole] * 5,
            scratch_shapes=[pltpu.VMEM((10, TILE, H), jnp.float32)],
        ),
        out_shape=[jax.ShapeDtypeStruct((ROWS, H), jnp.float32)] * 5,
        compiler_params=params(),
        cost_estimate=SHORT,
        name="gather_terms",
    )(info, *([in_hbm(tiles)] * n), *fields, *before)


def dense_kernel(own, *refs):
    got, (weight, bias, cotangent, agg, output, grad_pre, grad_agg) = refs[:-7], refs[-7:]
    total = own[...]
    for ref in got:
        total += ref[...]
    agg[...] = total
    weight_high, weight_low = split(weight[...])
    value = dot3(*split(total), weight_high, weight_low) + bias[...]
    scale = 0.7978845608028654
    square = value * value
    turn = jnp.tanh(scale * (value + 0.044715 * (square * value)))
    half = 0.5 * (1.0 + turn)
    output[...] = value * half
    slope = half + 0.5 * value * (1.0 - turn * turn) * (scale * (1.0 + 3.0 * 0.044715 * square))
    grad = cotangent[...] * slope
    grad_pre[...] = grad
    turned_high, turned_low = split(weight[...].T)
    grad_agg[...] = dot3(*split(grad), turned_high, turned_low)


def dense(own, got, weight, bias, cotangent):
    return pl.pallas_call(
        dense_kernel,
        out_shape=[jax.ShapeDtypeStruct((ROWS, H), jnp.float32)] * 4,
        compiler_params=params(),
        cost_estimate=cost(12 * 256 * 256 * 256, 10 * 256 * 1024),
        name="dense",
    )(own, *got, weight, bias.reshape(1, H), cotangent)


def weight_kernel(agg, grad_pre, weight_term, bias_term):
    weight_term[...] = dot3(*split(agg[...].T), *split(grad_pre[...]))
    total = jnp.sum(grad_pre[...], axis=0, keepdims=True)
    wide = H // PART
    bias_term[...] = jnp.zeros_like(bias_term)
    for j in range(PART):
        bias_term[j : j + 1, :wide] = total[:, j * wide : (j + 1) * wide]


def weight_terms(agg, grad_pre):
    return pl.pallas_call(
        weight_kernel,
        out_shape=[
            pltpu.HBM((H, H), jnp.float32),
            jax.ShapeDtypeStruct((PART, 128), jnp.float32),
        ],
        compiler_params=params(),
        cost_estimate=cost(6 * 256 * 256 * 256, 3 * 256 * 1024),
        name="weight_terms",
    )(agg, grad_pre)


def spread_kernel(at, n, info, *refs):
    highs, lows = refs[:n], refs[n : 2 * n]
    band, outs, (band_high, band_low) = refs[2 * n : 2 * n + 5], refs[2 * n + 5 : -2], refs[-2:]
    for j, ref in enumerate(band):
        high, low = split(ref[...])
        band_high[2 * j : 2 * j + 2] = high.reshape(2, TILE, H)
        band_low[2 * j : 2 * j + 2] = low.reshape(2, TILE, H)
    for j in range(n):
        chosen = [band_row(info, info[at + j], slot) for slot in range(PER_BLOCK)]
        chosen_high = jnp.concatenate([band_high[row] for row in chosen], axis=0)
        chosen_low = jnp.concatenate([band_low[row] for row in chosen], axis=0)
        product = dot3(highs[j][0], lows[j][0], chosen_high, chosen_low)
        if len(outs) == 1:
            outs[0][j] = product
        else:
            outs[j][...] = product


def spread_terms(at, n, info, high_t, low_t, band, apart=False):
    whole = pl.BlockSpec((ROWS, H), lambda i, *_: (0, 0))
    tiles = [
        pl.BlockSpec((1, ROWS, PER_BLOCK * TILE), lambda i, info, j=j: (info[at + j], 0, 0)) for j in range(n)
    ]
    return pl.pallas_call(
        functools.partial(spread_kernel, at, n),
        grid_spec=pltpu.PrefetchScalarGridSpec(
            num_scalar_prefetch=1,
            grid=(1,),
            in_specs=tiles * 2 + [whole] * 5,
            out_specs=[whole] * n if apart else pl.BlockSpec((n, ROWS, H), lambda i, *_: (0, 0, 0)),
            scratch_shapes=[pltpu.VMEM((10, TILE, H), jnp.bfloat16)] * 2,
        ),
        out_shape=[pltpu.HBM((ROWS, H), jnp.float32)] * n if apart else pltpu.HBM((n, ROWS, H), jnp.float32),
        compiler_params=params(),
        cost_estimate=LONG,
        name="spread_terms",
    )(info, *([in_hbm(high_t)] * n), *([in_hbm(low_t)] * n), *band)


def turn_kernel(kept_first, given_first, far, kept, given, second, passed, held):
    passed[...] = kept_first[...] + given_first[0] + far[...]
    held[...] = kept[...] + given[0] + second[...]


def turn_terms(kept_first, kept, given, far, second):
    whole = pl.BlockSpec((ROWS, H), lambda i: (0, 0))
    return pl.pallas_call(
        turn_kernel,
        grid=(1,),
        in_specs=[
            whole,
            pl.BlockSpec((1, ROWS, H), lambda i: (1, 0, 0)),
            whole,
            whole,
            pl.BlockSpec((1, ROWS, H), lambda i: (3, 0, 0)),
            whole,
        ],
        out_specs=[whole, whole],
        out_shape=[jax.ShapeDtypeStruct((ROWS, H), jnp.float32)] * 2,
        compiler_params=params(),
        cost_estimate=LONG,
        name="turn_terms",
    )(kept_first, given, far, kept, given, second)


def other_core(value):
    return lax.ppermute(value, "core", [(0, 1), (1, 0)])


def along_loop(value, sign):
    pairs = []
    for z in range(Z_HI):
        for core in range(CORE):
            by = sign if core == 0 else -sign
            pairs.append((z * CORE + core, (z + by) % Z_HI * CORE + core))
    return lax.ppermute(value, LOOP, pairs)


def in_triple(value, by):
    return lax.ppermute(value, "z_lo", [(i, (i + by) % Z_LO) for i in range(Z_LO)])


def across_triples(value, by):
    pairs = [(r, (r + Z_LO * by[r % Z_LO]) % N_REP) for r in range(N_REP)]
    return lax.ppermute(value, REP, pairs)


def swap(value, axes):
    return lax.all_to_all(value, axes, 0, 0, tiled=True)


def copy_kernel(parts, bias_part, out):
    total = jnp.sum(parts[...], axis=0)
    if bias_part is not None:
        total = jnp.concatenate([total, bias_part[...]], axis=1)
    for j in range(out.shape[0]):
        out[j] = total


def sum_and_copy(parts, copies, bias_part=None):
    width = parts.shape[2] + (0 if bias_part is None else bias_part.shape[1])
    if bias_part is None:
        kernel = lambda parts, out: copy_kernel(parts, None, out)
    else:
        kernel = copy_kernel
    return pl.pallas_call(
        kernel,
        out_shape=jax.ShapeDtypeStruct((copies, PART, width), jnp.float32),
        compiler_params=params(),
        cost_estimate=cost(1 << 10, 1 << 10),
        name="sum_and_copy",
    )(*((parts,) if bias_part is None else (parts, bias_part)))


def read_kernel(whole, weight_whole, bias_whole):
    for j in range(N_PLANE):
        weight_whole[j * PART : (j + 1) * PART, :] = whole[j, :, :H] / NODES
    bias_part = jnp.sum(whole[:, :, H:], axis=0) / NODES
    wide = H // PART
    for j in range(PART):
        bias_whole[:, j * wide : (j + 1) * wide] = bias_part[j : j + 1, :wide]


def read_sums(whole):
    weight_whole, bias_whole = pl.pallas_call(
        read_kernel,
        out_shape=[jax.ShapeDtypeStruct((H, H), jnp.float32), jax.ShapeDtypeStruct((1, H), jnp.float32)],
        compiler_params=params(),
        name="read_sums",
    )(whole)
    return weight_whole, bias_whole.reshape(H)


def after(value, *others):
    return lax.optimization_barrier((value,) + others)


def per_device(features, weight, bias, tile_values, tile_rows, tile_cols, tile_counts, cotangent):
    z_hi, core, z_lo = lax.axis_index("z_hi"), lax.axis_index("core"), lax.axis_index("z_lo")

    turn = 1 - 2 * core
    first = (z_hi - turn) % Z_HI
    second = (z_hi + turn) % Z_HI
    far = (z_hi + 2) % Z_HI

    def block(z, c):
        return z * CORE + c

    blocks = [
        block(z_hi, core),
        block(z_hi, 1 - core),
        block(first, core),
        block(second, 1 - core),
        block(second, core),
        block(first, 1 - core),
        block(far, core),
        block(far, 1 - core),
        block(far, 1 - core),
        block(second, 1 - core),
        block(first, 1 - core),
        block(z_hi, 1 - core),
        block(far, core),
        block(first, core),
        block(second, core),
        block(z_hi, core),
    ]
    places = [
        jnp.where(z_lo == 0, line[0], jnp.where(z_lo == 1, line[1], line[2])) for line in zip(*BAND_PLACE)
    ]
    (scalars,) = after(jnp.stack(blocks + places))
    info = jnp.concatenate([scalars, tile_rows[0], tile_cols[0], tile_counts[0]])

    first_upper = along_loop(features[:TILE], 1)
    first_lower = along_loop(features[TILE:], 1)
    second_payload, info = after(features, info)
    field_second = along_loop(second_payload, -1)
    first_upper, own_field, info = after(first_upper, features, info)
    field_other = other_core(own_field)
    far_upper = along_loop(first_upper, 1)
    far_lower = along_loop(first_lower, 1)
    field_first = jnp.concatenate([first_upper, first_lower])
    field_far = jnp.concatenate([far_upper, far_lower])
    other_first = other_core(field_first)
    terms = gather_terms(GATHER_NEAR, info, tile_values[0], (in_hbm(features), field_other, field_first))
    far_upper, field_second, *terms = after(far_upper, field_second, *terms)
    other_second = other_core(field_second)
    other_far = other_core(field_far)
    terms = gather_terms(GATHER_MIDDLE, info, tile_values[0], (other_first, field_second, other_second), terms)
    own, term_a, term_b, term_y1, term_y2 = gather_terms(
        GATHER_FAR, info, tile_values[0], (field_far, other_far), terms
    )

    high_t, low_t = place_tiles(info, tile_values[0])
    got_y1 = across_triples(term_y1, (-1, -1, 1))
    got_y2 = across_triples(term_y2, (-1, 1, 1))
    got_a = in_triple(term_a + got_y1, 1)
    got_b = in_triple(term_b + got_y2, 2)
    got_a, got_b, high_t, low_t = after(got_a, got_b, high_t, low_t)
    agg, output, grad_pre, grad_agg = dense(own, (got_a, got_b), weight, bias, cotangent)
    band_a = in_triple(grad_agg, -1)
    band_b = in_triple(grad_agg, -2)
    weight_term, bias_term = weight_terms(agg, grad_pre)
    band_a, band_b, _ = after(band_a, band_b, weight_term)
    band_y1 = across_triples(band_a, (1, 1, -1))
    band_y2 = across_triples(band_b, (1, -1, -1))
    sums = swap(weight_term.reshape(N_PLANE, PART, H), PLANE)
    sums = sum_and_copy(sums, N_COLUMN, bias_term)
    band = (grad_agg, band_a, band_b, band_y1, band_y2)
    sums = sum_and_copy(swap(sums, COLUMN), N_PLANE)

    given = other_core(spread_terms(SPREAD_OTHER, 4, info, high_t, low_t, band))
    kept_far, kept_first, kept_second, kept = spread_terms(SPREAD_OWN, 4, info, high_t, low_t, band, apart=True)
    got_far = along_loop(kept_far + given[0], -1)
    got_second = along_loop(kept_second + given[2], 1)
    passed, held = turn_terms(kept_first, kept, given, got_far, got_second)
    weight_whole, bias_whole = read_sums(swap(sums, PLANE))
    held, weight_whole, bias_whole = after(held, weight_whole, bias_whole)
    grad_features = held + along_loop(passed, -1)
    return (output, grad_features, weight_whole, bias_whole)


def solution(mesh):
    cut = Mesh(mesh.devices.reshape(Z_HI, CORE, X, Y, Z_LO), AXES)
    nodes = P(AXES)
    return jax.shard_map(
        per_device,
        mesh=cut,
        in_specs=(nodes, P(), P(), nodes, nodes, nodes, nodes, nodes),
        out_specs=(nodes, nodes, P(), P()),
        check_vma=False,
    )
```
